256 devices in a mesh: blk: 16 (over y_hi, x, core), tile: 16 (over y_lo, z).
Axes of the slice: x: 4, y: 4 (y_hi: 2, y_lo: 2; y = y_hi * 2 + y_lo), z: 8, core: 2. Of those that a mesh axis runs over, the one named last changes fastest.
Arguments:
- images: bfloat16 [32768, 512], P(('blk', 'tile')), may hold values from -6 to 6
- texts: bfloat16 [32768, 512], P(('blk', 'tile')), may hold values from -6 to 6
- teacher_codes: bfloat16 [32768, 16, 2048], P('blk', None, 'tile'), may hold values from -4 to 4
- teacher_scales: float32 [256, 16, 16], P('blk', None, 'tile'), may hold values from 0.5 to 4
- student_logit_scale: float32 [1], replicated, may hold values from 2 to 6
- logit_bias: float32 [1], replicated, may hold values from -3 to 0
Outputs:
- grad_images: float32 [32768, 512], P(('blk', 'tile'))
- grad_texts: float32 [32768, 512], P(('blk', 'tile'))
The draws below stay inside these ranges and needn't reach their ends.
All inputs are finite; a program needn't handle non-finite values.
Results may differ from the reference program's by a relative error of at most 0.0044.
Values may be sent and summed in bfloat16 or wider, within the bound.
A program may use at most 128 MiB of HBM per device.

```python
import math
import jax
import jax.numpy as jnp
from jax import lax

E = 512
QT = 128
ROWS_DEV = 128
TEXT_BLOCK = 2048
BATCH = 32768
N_BLK = 16
N_TILE = 16


def shard_levels(own_key, dims, split, smallest, top_value):
    def one(axis_at, shards_of):
        draws = jax.random.uniform(jax.random.fold_in(jax.random.fold_in(own_key, 6), axis_at), (shards_of,), jnp.float32, smallest / len(split), top_value / len(split))
        return jnp.repeat(jnp.exp(draws), dims[axis_at] // shards_of).reshape((-1,) + (1,) * (len(dims) - axis_at - 1))

    factor_of = one(*split[0])
    for cut in split[1:]:
        factor_of = factor_of * one(*cut)
    return factor_of


def normal_values(rng, extent, deviation, reach, shards=(), held_as=jnp.bfloat16):
    loudness = shard_levels(rng, extent, shards, -0.22, 0.18) if shards else 1.0
    result = jax.random.normal(rng, extent, jnp.float32) * deviation * loudness
    return jnp.minimum(jnp.maximum(result, -reach), reach).astype(held_as)


def setup_inputs(seed: int = 0) -> dict:
    keys = jax.random.split(jax.random.key(seed), 7)
    return {
        "images": normal_values(keys[0], (BATCH, E), 1.0, 6.0, ((0, 256),)),
        "texts": normal_values(keys[1], (BATCH, E), 1.0, 6.0, ((0, 256),)),
        "teacher_codes": normal_values(keys[2], (BATCH, N_BLK, TEXT_BLOCK), 1.0, 4.0, ((0, 16), (2, 16))),
        "teacher_scales": jnp.clip(jnp.exp(math.log(4.0) - 2.0794415 * jax.random.uniform(keys[3], (BATCH // QT, N_BLK, TEXT_BLOCK // QT), jnp.float32) ** shard_levels(keys[3], (BATCH // QT, N_BLK, TEXT_BLOCK // QT), ((0, 16), (2, 16)), -0.2, 0.2)), 0.5, 4.0),
        "student_logit_scale": jnp.clip(jax.random.uniform(keys[4], (1,), jnp.float32, 2.0, 6.0), 2.0, 6.0),
        "logit_bias": jnp.clip(jax.random.uniform(keys[5], (1,), jnp.float32, -3.0, 0.0), -3.0, 0.0),
    }


epsilon = 1e-06

def unit_rows(embedded):
    values = embedded.astype(jnp.float32)
    magnitude = jnp.sqrt(lax.optimization_barrier(jnp.sum(values * values, axis=-1, keepdims=True)) + epsilon)
    return (values / magnitude, magnitude)

def unit_grad(grad_unit, unit_vectors, magnitude):
    inner = lax.optimization_barrier(jnp.sum(unit_vectors * grad_unit, axis=-1, keepdims=True))
    return (grad_unit - unit_vectors * inner) / magnitude

def reference(images, texts, teacher_codes, teacher_scales, student_logit_scale, logit_bias):
    image_unit, image_norm = unit_rows(images)
    text_unit, text_norm = unit_rows(texts)
    image_low = image_unit.astype(jnp.bfloat16)
    caption_lower = text_unit.astype(jnp.bfloat16)
    softness_level = student_logit_scale[0]
    offset_term = logit_bias[0]
    block_rows = ROWS_DEV * N_TILE

    def one_block(gradient_caption, block_index):
        offset = (block_index * block_rows).astype(jnp.int32)
        tile_offset = (block_index * (block_rows // QT)).astype(jnp.int32)
        picture_block = lax.dynamic_slice_in_dim(image_low, offset, block_rows, 0)
        code_block = lax.dynamic_slice_in_dim(teacher_codes, offset, block_rows, 0)
        scale_block = lax.dynamic_slice_in_dim(teacher_scales, tile_offset, block_rows // QT, 0)
        teacher = code_block.astype(jnp.float32).reshape(block_rows // QT, QT, N_BLK, block_rows // QT, QT)
        teacher = (teacher * scale_block[:, None, :, :, None]).reshape(block_rows, N_BLK * block_rows)
        student_model = softness_level * jnp.dot(picture_block, caption_lower.T, preferred_element_type=jnp.float32) + offset_term
        pair_weight = (jax.nn.sigmoid(student_model) - jax.nn.sigmoid(teacher)).astype(jnp.bfloat16)
        gradient_tile = softness_level * jnp.dot(pair_weight, caption_lower, preferred_element_type=jnp.float32)
        gradient_caption = gradient_caption + softness_level * jnp.dot(pair_weight.T, picture_block, preferred_element_type=jnp.float32)
        return (gradient_caption, gradient_tile)
    grad_text_unit, blocks = lax.scan(one_block, jnp.zeros((BATCH, E), jnp.float32), jnp.arange(N_BLK, dtype=jnp.int32))
    grad_image_unit = blocks.reshape(BATCH, E)
    return (unit_grad(grad_image_unit, image_unit, image_norm), unit_grad(grad_text_unit, text_unit, text_norm))
```

```python
import jax
import jax.numpy as jnp
from jax import lax
from jax.experimental import pallas as pl
from jax.experimental.pallas import tpu as pltpu
from jax.sharding import PartitionSpec as P

EPS = 1e-06
F32 = jnp.float32
BF = jnp.bfloat16
R = 128
E = 512
NZ = 8
NX = 4
NC = 16


def unit_rows(values):
    magnitude = jnp.sqrt(jnp.sum(values * values, axis=-1, keepdims=True) + EPS)
    return values / magnitude, magnitude


def unit_grad(grad_unit, unit_vectors, magnitude):
    inner = jnp.sum(unit_vectors * grad_unit, axis=-1, keepdims=True)
    return (grad_unit - unit_vectors * inner) / magnitude


PLUS = ((4, 0, None), (3, 1, None), (3, 0, 0), (2, 1, 1), (2, 0, 2), (1, 1, 3), (1, 0, 4))
MINUS = ((4, 0, None), (3, 1, None), (3, 0, 0), (2, 1, 1), (2, 0, 2), (1, 0, 4), (1, 1, 3))


def kernel(
    img_ref, txt_ref, codes_ref, scales_ref, scale_ref, bias_ref,
    dimg_ref, dtxt_ref,
    codes, scb, pt, J, T, dI, dT,
    js, jr, ds_, dr, xs, xr, fs, fr,
    codes_sem, jsend, jrecv, tsend, trecv, isend, irecv, dsend, drecv, xsend, xrecv, fsend, frecv,
):
    bi, ti = lax.axis_index("blk"), lax.axis_index("tile")
    h, x, k = bi // 8, (bi // 2) % NX, bi % 2
    l, z = ti // NZ, ti % NZ

    def blk(hh, xx, kk):
        return hh * 8 + ((xx + 8) % NX) * 2 + kk

    def zz(d):
        return (z + d + 16) % NZ

    up, down = {"tile": l * NZ + zz(1)}, {"tile": l * NZ + zz(-1)}
    ylo = {"tile": (1 - l) * NZ + z}
    yhi = {"blk": blk(1 - h, x, k)}
    right, left = {"blk": blk(h, x + 1, k)}, {"blk": blk(h, x - 1, k)}
    core = {"blk": blk(h, x, 1 - k)}

    def codes_copy(r):
        rows = pl.ds(r * R, R)
        return pltpu.make_async_copy(codes_ref.at[rows], codes.at[rows], codes_sem.at[r])

    for r in range(NC):
        codes_copy(r).start()

    barrier = pltpu.get_barrier_semaphore()
    for dev in (up, down, ylo, yhi, right, left, core):
        pl.semaphore_signal(barrier, inc=1, device_id=dev, device_id_type=pl.DeviceIdType.MESH)

    def remote(src, dst, send, recv, dev):
        return pltpu.make_async_remote_copy(
            src_ref=src, dst_ref=dst, send_sem=send, recv_sem=recv, device_id=dev,
            device_id_type=pl.DeviceIdType.MESH,
        )

    def j_copy(i):
        if i == 14:
            return remote(J.at[z, l], J.at[z, l], jsend.at[i], jrecv.at[i], ylo)
        n, sign = (i, 1) if i < 7 else (i - 7, -1)
        if n == 6:
            col = l if sign == 1 else 1 - l
        else:
            col = l if n % 2 == 0 else 1 - l
        spot = J.at[zz(-sign * (n // 2)), col]
        return remote(spot, spot, jsend.at[i], jrecv.at[i], up if sign == 1 else down)

    def j_recv(i):
        j_copy(i).wait_recv()

    def t_copy(i):
        n = i % 3
        if i < 3:
            spot, dev = (T.at[blk(h, x, k)], T.at[blk(1 - h, x, k)], T.at[blk(h, x - 1, k)])[n], right
        elif i < 6:
            spot, dev = (T.at[blk(h, x, k)], T.at[blk(1 - h, x, k)], T.at[blk(1 - h, x + 1, k)])[n], left
        elif i == 6:
            spot, dev = T.at[bi], yhi
        else:
            m = i - 7
            spot, dev = T.at[blk(h if m % 2 == 0 else 1 - h, x + (0, -1, 1, 2)[m // 2], k)], core
        return remote(spot, spot, tsend.at[i], trecv.at[i], dev)

    def t_recv(i):
        t_copy(i).wait_recv()

    img_unit, _ = unit_rows(img_ref[...].astype(F32))
    txt_unit, _ = unit_rows(txt_ref[...].astype(F32))
    J[z, l] = img_unit.astype(BF)
    T[bi] = txt_unit.astype(BF)

    pl.semaphore_wait(barrier, 7)
    for i in (0, 7, 14):
        j_copy(i).start()
    for i in (0, 3, 6, 7):
        t_copy(i).start()

    eye = lax.broadcasted_iota(jnp.int32, (NC, NC), 0) == lax.broadcasted_iota(jnp.int32, (NC, NC), 1)
    for r in range(NC):
        row = jnp.broadcast_to(scales_ref[r], (NC, NC))
        column = jnp.sum(jnp.where(eye, row, 0.0), axis=-1, keepdims=True)
        scb[r] = jnp.broadcast_to(0.5 * column, (NC, R))

    def teacher_rows(r, carry):
        codes_copy(r).wait()
        sc = scb[r]

        def some(g, inner):
            for u in range(16):
                i = r * R + g * 16 + u
                pt[pl.ds(pl.multiple_of(i * NC, NC), NC), :] = jnp.tanh(codes[i].astype(F32) * sc)
            return inner

        return lax.fori_loop(0, R // 16, some, carry)

    lax.fori_loop(0, 8, teacher_rows, 0)
    j_recv(14)
    j_copy(1).start()
    j_copy(8).start()
    t_recv(6)
    for i in (1, 4, 8):
        t_copy(i).start()
    t_recv(0)
    t_copy(9).start()
    t_copy(2).start()
    t_recv(3)
    t_copy(11).start()
    for i in (0, 7):
        j_recv(i)
        j_copy(i + 2).start()
    lax.fori_loop(8, 16, teacher_rows, 0)
    t_recv(1)
    t_copy(10).start()
    t_recv(4)
    t_copy(12).start()
    t_copy(5).start()
    for i in (1, 8):
        j_recv(i)
        j_copy(i + 2).start()
    t_recv(2)
    t_copy(13).start()
    t_recv(5)
    t_copy(14).start()
    for i in range(7, 15):
        t_recv(i)

    half_scale = 0.5 * scale_ref[0]
    half_bias = 0.5 * bias_ref[0]
    dT[...] = jnp.zeros_like(dT)

    def pairs(zb):
        rows = J[zb].reshape(2 * R, E)
        texts = T[...].reshape(NC * R, E)
        score = lax.dot_general(rows, texts, (((1,), (1,)), ((), ())), preferred_element_type=F32)
        parts = []
        for a in range(2):
            first = (a * NZ + zb) * (R * NC)
            cells = []
            for c in range(NC):
                teacher = pt[pl.ds(first + c, R, stride=NC), :]
                s = score[a * R:(a + 1) * R, c * R:(c + 1) * R]
                cells.append((jnp.tanh(s * half_scale + half_bias) - teacher).astype(BF))
            parts.append(jnp.concatenate(cells, axis=1))
        weight = jnp.concatenate(parts, axis=0)
        dI[zb] = jnp.dot(weight, texts, preferred_element_type=F32).reshape(2, R, E)
        dT[...] += lax.dot_general(
            weight, rows, (((0,), (0,)), ((), ())), preferred_element_type=F32
        ).reshape(NC, R, E)

    def i_send(sign, n):
        table = PLUS if sign == 1 else MINUS
        base = 0 if sign == 1 else 7
        dist, other, dep = table[n]
        a = l if sign == 1 else 1 - l
        col = 1 - a if other else a
        value = dI[zz(sign * dist), col]
        if dep is not None:
            i_copy(sign, dep).wait_recv()
            value = value + jr[base + dep].astype(F32)
        js[base + n] = value.astype(BF)
        i_copy(sign, n).start()

    def i_copy(sign, n):
        i = n if sign == 1 else 7 + n
        return remote(js.at[i], jr.at[i], isend.at[i], irecv.at[i], up if sign == 1 else down)

    order = (0, 1, -1, 2, 4, 3, -3, -2)

    def step(s, carry):
        @pl.when(s == 0)
        def _():
            for i in (2, 9):
                j_recv(i)
                j_copy(i + 2).start()

        @pl.when(s == 1)
        def _():
            for i in (3, 10):
                j_recv(i)
                j_copy(i + 2).start()

        @pl.when(s == 2)
        def _():
            j_recv(4)
            j_copy(6).start()
            j_recv(11)

        @pl.when(s == 3)
        def _():
            j_recv(12)
            j_copy(13).start()
            j_recv(5)

        @pl.when(s == 4)
        def _():
            j_recv(6)
            j_recv(13)

        @pl.when(s == 5)
        def _():
            i_send(1, 0)
            i_send(-1, 0)

        @pl.when(s == 6)
        def _():
            i_send(1, 1)
            i_send(1, 2)

        @pl.when(s == 7)
        def _():
            i_send(-1, 1)
            i_send(-1, 2)

        zb = jnp.int32(0)
        for n, d in enumerate(order):
            zb = jnp.where(s == n, zz(d), zb)
        pairs(zb)
        return carry

    lax.fori_loop(0, NZ, step, 0)

    spots = tuple((hh, dx) for dx in (2, 1, -1, 0) for hh in (0, 1))

    def d_copy(i):
        return remote(ds_.at[i], dr.at[i], dsend.at[i], drecv.at[i], core)

    def hcol(hh):
        return 1 - h if hh else h

    for i, (hh, dx) in enumerate(spots):
        ds_[i] = dT[blk(hcol(hh), x + dx, 1 - k)].astype(BF)
        d_copy(i).start()

    i_send(1, 3)
    i_send(-1, 3)

    def chip_sum(hh, dx):
        i = spots.index((hh, dx))
        d_copy(i).wait_recv()
        return dT[blk(hcol(hh), x + dx, k)] + dr[i].astype(F32)

    def x_copy(i):
        return remote(xs.at[i], xr.at[i], xsend.at[i], xrecv.at[i], right if i < 3 else left)

    def x_send(i, value):
        xs[i] = value.astype(BF)
        x_copy(i).start()

    def x_recv(i):
        x_copy(i).wait_recv()
        return xr[i].astype(F32)

    x_send(0, chip_sum(0, 2))
    x_send(3, chip_sum(1, 2))
    x_send(1, chip_sum(1, 1))
    x_send(4, chip_sum(0, -1))
    i_send(1, 4)
    i_send(-1, 4)
    x_send(2, chip_sum(0, 1) + x_recv(0))
    x_send(5, chip_sum(1, -1) + x_recv(3))
    i_send(1, 5)
    i_send(-1, 5)
    i_send(1, 6)
    i_send(-1, 6)

    def f_copy(i):
        return remote(fs.at[i], fr.at[i], fsend.at[i], frecv.at[i], yhi if i else ylo)

    fs[1] = (chip_sum(1, 0) + x_recv(1) + x_recv(5)).astype(BF)
    f_copy(1).start()
    own_text = chip_sum(0, 0) + x_recv(2) + x_recv(4)

    def i_recv(sign, n):
        i_copy(sign, n).wait_recv()
        return jr[n if sign == 1 else 7 + n].astype(F32)

    fs[0] = (dI[z, 1 - l] + i_recv(1, 5) + i_recv(-1, 5)).astype(BF)
    f_copy(0).start()

    f_copy(1).wait_recv()
    unit, mag = unit_rows(txt_ref[...].astype(F32))
    dtxt_ref[...] = unit_grad(half_scale * (own_text + fr[1].astype(F32)), unit, mag)

    own_image = dI[z, l] + i_recv(1, 6) + i_recv(-1, 6)
    f_copy(0).wait_recv()
    unit, mag = unit_rows(img_ref[...].astype(F32))
    dimg_ref[...] = unit_grad(half_scale * (own_image + fr[0].astype(F32)), unit, mag)

    for i in range(15):
        j_copy(i).wait_send()
        t_copy(i).wait_send()
    for n in range(7):
        i_copy(1, n).wait_send()
        i_copy(-1, n).wait_send()
    for i in range(8):
        d_copy(i).wait_send()
    for i in range(6):
        x_copy(i).wait_send()
    for i in range(2):
        f_copy(i).wait_send()


def shards(images, texts, teacher_codes, teacher_scales, student_logit_scale, logit_bias):
    vmem = pl.BlockSpec(memory_space=pltpu.VMEM)
    smem = pl.BlockSpec(memory_space=pltpu.SMEM)
    row = lambda *n: pltpu.VMEM((*n, R, E), BF)
    dma = lambda n: pltpu.SemaphoreType.DMA((n,))
    return pl.pallas_call(
        kernel,
        out_shape=(jax.ShapeDtypeStruct((R, E), F32), jax.ShapeDtypeStruct((R, E), F32)),
        in_specs=[vmem, vmem, pl.BlockSpec(memory_space=pl.ANY), vmem, smem, smem],
        out_specs=(vmem, vmem),
        scratch_shapes=[
            pltpu.VMEM((NC * R, NC, R), BF),
            pltpu.VMEM((NC, NC, R), F32),
            pltpu.VMEM((NC * R * NC, R), F32),
            row(NZ, 2),
            row(NC),
            pltpu.VMEM((NZ, 2, R, E), F32),
            pltpu.VMEM((NC, R, E), F32),
            row(14), row(14), row(8), row(8), row(6), row(6), row(2), row(2),
            dma(NC), dma(15), dma(15), dma(15), dma(15), dma(14), dma(14),
            dma(8), dma(8), dma(6), dma(6), dma(2), dma(2),
        ],
        compiler_params=pltpu.CompilerParams(
            collective_id=0, has_side_effects=True, vmem_limit_bytes=60 * 1024 * 1024
        ),
    )(images, texts, teacher_codes, jnp.swapaxes(teacher_scales, 1, 2), student_logit_scale, logit_bias)


def solution(mesh):
    in_specs = (
        P(("blk", "tile"), None),
        P(("blk", "tile"), None),
        P("blk", None, "tile"),
        P("blk", None, "tile"),
        P(),
        P(),
    )
    out_specs = (P(("blk", "tile"), None), P(("blk", "tile"), None))
    return jax.shard_map(shards, mesh=mesh, in_specs=in_specs, out_specs=out_specs, check_vma=False)
```

```python
import jax
import jax.numpy as jnp
from jax import lax
from jax.experimental import pallas as pl
from jax.experimental.pallas import tpu as pltpu
from jax.sharding import PartitionSpec as P

EPS = 1e-06
F32 = jnp.float32
BF = jnp.bfloat16
R = 128
E = 512
NZ = 8
NX = 4
NC = 16
NH = 8
EARLY = 8
PIECES = {"": (0, R), "a": (0, R // 2), "b": (R // 2, R // 2)}

SCHEDULE = (
    "m0b", "xp0", "p0a", "yh", "xm0", "y0", "p0b", "c0", "m0a", "m1b", "p1a", "T", "m1a", "xp2a", "xm2b", "T",
    "T", "p1b", "c2", "xp1", "xm1", "m3b", "c4", "p3a", "T", "T", "y1", "c1", "m2", "p2", "T", "c3", "T", "T",
    "p3b", "y2", "m3a", "m4b", "p4a", "xp3a", "xm3b", "c6", "c5", (0, 0), "m5", (0, 2), (0, -1), "c7", (0, 1),
    (1, 1), "y3", "p5", (1, 2), "q4", (1, -1), (0, 3), (1, 3), "r4", "q5", (0, 4), (1, 4), "k2a", (1, -3),
    "k2b", (0, -3), "r5", (1, 0), (1, -2), "q0a", "k0a", "d7", "r0b", "d6", "k0b", "q1b", "r1a", "u10a",
    "v10b", (0, -2), "k1a", "u11b", "d5", "q1a", "d3", "r1b", "k1b", "v11a", "q2b", "u11a", "k3", "v11b",
    "u00a", "r2a", "d1", "d4", "d2", "v00b", "q2a", "r2b", "fa", "u01b", "q3b", "v01a", "r3a", "fb", "u01a",
    "v01b", "q3a", "r3b", "d0",
)
NEEDS = {
    "p1a": ("p0a",), "p1b": ("p0b",), "m1a": ("m0a",), "m1b": ("m0b",), "p2": ("y0",), "m2": ("y0",),
    "p3a": ("p1a",), "p3b": ("p1b",), "m3a": ("m1a",), "m3b": ("m1b",), "p4a": ("p3a",), "m4b": ("m3b",),
    "y1": ("m1a", "m1b"), "y2": ("p1a", "p1b"), "p5": ("y2",), "m5": ("y1",), "y3": ("p4a", "m4b"),
    "xp2a": ("xp0",), "xm2b": ("xm0",), "c1": ("xp0",), "c2": ("xm0",), "c3": ("xp2a", "xm2b"),
    "c4": ("yh",), "xp1": ("yh",), "xm1": ("yh",), "c5": ("xp1",), "c6": ("xm1",),
    "xp3a": ("xp1",), "xm3b": ("xm1",), "c7": ("xp3a", "xm3b"),
    "k3": ("q4", "r4"), "q0a": ("k2a",), "r0b": ("k2b",), "q1a": ("q0a",), "r1b": ("r0b",),
    "k0a": ("q5",), "k0b": ("q5",), "k1a": ("r5",), "k1b": ("r5",),
    "q2a": ("k0a", "q1a"), "q2b": ("k0b", "q1b"), "r2a": ("k1a", "r1a"), "r2b": ("k1b", "r1b"),
    "q3a": ("q2a",), "q3b": ("q2b",), "r3a": ("r2a",), "r3b": ("r2b",),
    "u10a": ("d7",), "v10b": ("d7",), "u11a": ("d6", "u10a"), "u11b": ("d6",),
    "v11a": ("d5",), "v11b": ("d5", "v10b"), "fa": ("d4", "u11a", "v11a"), "fb": ("d4", "u11b", "v11b"),
    "u00a": ("d3",), "v00b": ("d3",), "u01a": ("d2", "u00a"), "u01b": ("d2",),
    "v01a": ("d1",), "v01b": ("d1", "v00b"),
}
IMAGES = {
    0: ("y0",), 1: ("m0a", "m0b", "m2"), -1: ("p0a", "p0b", "p2"), 2: ("m1a", "m1b", "y1"),
    -2: ("p1a", "p1b", "y2"), 3: ("m3a", "m3b", "m5"), -3: ("p3a", "p3b", "p5"), 4: ("p4a", "m4b", "y3"),
}
TEXTS = (
    ("c0", "c1", "c2", "c3", "xp0", "xm0", "xp2a", "xm2b"),
    ("yh", "xp1", "xm1", "xp3a", "xm3b", "c4", "c5", "c6", "c7"),
)
LAST_TEXT = ("d0", "u01a", "u01b", "v01a", "v01b", "fa", "fb")
LAST_IMAGE = ("k3", "q3a", "q3b", "r3a", "r3b")
SUMS = {
    "q0": (4, 0), "q1": (3, 0), "q2": (2, 0), "q3": (1, 0), "q4": (1, 1), "q5": (3, 1),
    "r0": (4, 0), "r1": (-3, 0), "r2": (-2, 0), "r3": (-1, 0), "r4": (-1, 1), "r5": (-3, 1),
    "k0": (2, 1), "k1": (-2, 1), "k2": (4, 1), "k3": (0, 1),
}
SPOTS = ((0, 0), (0, -1), (0, 1), (0, 2), (1, 0), (1, -1), (1, 1), (1, 2))
X_SPOTS = {"u0": 3, "v0": 3, "u1": 2, "v1": 1}
COPIES = tuple(n for n in SCHEDULE if isinstance(n, str) and n != "T")
TILES = tuple(n for n in SCHEDULE if not isinstance(n, str))


def split(name):
    piece = name[-1] if name[-1] in "ab" else ""
    return name[: len(name) - len(piece)], pl.ds(*PIECES[piece])


def unit_rows(values):
    magnitude = jnp.sqrt(jnp.sum(values * values, axis=-1, keepdims=True) + EPS)
    return values / magnitude, magnitude


def unit_grad(grad_unit, unit_vectors, magnitude):
    inner = jnp.sum(unit_vectors * grad_unit, axis=-1, keepdims=True)
    return (grad_unit - unit_vectors * inner) / magnitude


def kernel(
    img_ref, txt_ref, codes_ref, scales_ref, scale_ref, bias_ref,
    dimg_ref, dtxt_ref,
    codes, scb, pt, J, T, dI, dT, zs, zr, ks, kr, ds_, dr, xs, xr, fs, fr,
    codes_sem, ssem, rsem,
):
    bi, ti = lax.axis_index("blk"), lax.axis_index("tile")
    h, x, k = bi // 8, (bi // 2) % NX, bi % 2
    l, z = ti // NZ, ti % NZ

    def blk(hh, xx, kk):
        return hh * 8 + ((xx + 8) % NX) * 2 + kk

    def zz(d):
        return (z + d + 16) % NZ

    def hcol(other):
        return 1 - h if other else h

    def lcol(other):
        return 1 - l if other else l

    up, down = {"tile": l * NZ + zz(1)}, {"tile": l * NZ + zz(-1)}
    ylo = {"tile": (1 - l) * NZ + z}
    yhi = {"blk": blk(1 - h, x, k)}
    right, left = {"blk": blk(h, x + 1, k)}, {"blk": blk(h, x - 1, k)}
    core = {"blk": blk(h, x, 1 - k)}

    def codes_copy(r):
        rows = pl.ds(r * R, R)
        return pltpu.make_async_copy(codes_ref.at[rows], codes.at[rows], codes_sem.at[r])

    barrier = pltpu.get_barrier_semaphore()
    for dev in (up, down, ylo, yhi, right, left, core):
        pl.semaphore_signal(barrier, inc=1, device_id=dev, device_id_type=pl.DeviceIdType.MESH)
    for r in range(NC):
        codes_copy(r).start()

    def landing(name):
        base, rows = split(name)
        i = int(base[1]) if base[0] in "qrkdu" or base[0] == "v" else 0
        if base[0] in "qr":
            return zs, zr, i if base[0] == "q" else 6 + i, rows
        if base[0] == "k":
            return ks, kr, i, rows
        if base[0] == "d":
            return ds_, dr, i, rows
        if base[0] == "f":
            return fs, fr, 0, rows
        return xs, xr, i * 4 + int(base[2]) * 2 + (base[0] == "v"), rows

    def copy(name):
        base, rows = split(name)
        kind = base[0]
        if kind in "pmy" and base != "yh":
            n = int(base[1])
            dz = {"p": (0, -1, 0, -2, -3, -2), "m": (0, 1, 0, 2, 3, 2), "y": (0, 2, -2, 4)}[kind][n]
            spot = J.at[zz(dz), lcol(kind != "y" and n in (2, 5)), rows]
            src, dst, dev = spot, spot, {"p": up, "m": down, "y": ylo}[kind]
        elif kind in "xyc":
            if base == "yh":
                spot, dev = T.at[bi, rows], yhi
            elif kind == "c":
                hh, dx = SPOTS[int(base[1])]
                spot, dev = T.at[blk(hcol(hh), x + dx, k), rows], core
            else:
                n, sign = int(base[2]), 1 if base[1] == "p" else -1
                spot = T.at[blk(hcol(n % 2), x - sign if n >= 2 else x, k), rows]
                dev = right if sign == 1 else left
            src, dst = spot, spot
        else:
            out, into, i, rows = landing(name)
            src, dst = out.at[i, rows], into.at[i, rows]
            dev = {"q": up, "r": down, "k": ylo, "d": core, "u": right, "v": left, "f": yhi}[kind]
        i = COPIES.index(name)
        return pltpu.make_async_remote_copy(
            src_ref=src, dst_ref=dst, send_sem=ssem.at[i], recv_sem=rsem.at[i], device_id=dev,
            device_id_type=pl.DeviceIdType.MESH,
        )

    seen = set()

    def arrive(names):
        for name in names:
            if name not in seen:
                seen.add(name)
                copy(name).wait_recv()

    img_unit, _ = unit_rows(img_ref[...].astype(F32))
    J[z, l] = img_unit.astype(BF)
    txt_unit, _ = unit_rows(txt_ref[...].astype(F32))
    T[bi] = txt_unit.astype(BF)

    eye = lax.broadcasted_iota(jnp.int32, (NC, NC), 0) == lax.broadcasted_iota(jnp.int32, (NC, NC), 1)
    for r in range(NC):
        row = jnp.broadcast_to(scales_ref[r], (NC, NC))
        column = jnp.sum(jnp.where(eye, row, 0.0), axis=-1, keepdims=True)
        scb[r] = jnp.broadcast_to(0.5 * column, (NC, R))

    def teacher_rows(r, carry):
        codes_copy(r).wait()
        sc = scb[r]
        dT[r] = jnp.zeros((R, E), F32)
        dI[r // 2, r % 2] = jnp.zeros((R, E), F32)

        def some(g, inner):
            for u in range(16):
                i = r * R + g * 16 + u
                pt[pl.ds(pl.multiple_of(i * NC, NC), NC), :] = jnp.tanh(codes[i].astype(F32) * sc)
            return inner

        return lax.fori_loop(0, R // 16, some, carry)

    half_scale = 0.5 * scale_ref[0]
    half_bias = 0.5 * bias_ref[0]

    def pairs(zb, hb):
        rows = J[zb].reshape(2 * R, E)
        columns = pl.ds(hb * NH, NH)
        texts = T[columns].reshape(NH * R, E)
        score = lax.dot_general(rows, texts, (((1,), (1,)), ((), ())), preferred_element_type=F32)
        parts = []
        for a in range(2):
            first = (a * NZ + zb) * (R * NC) + hb * NH
            cells = []
            for c in range(NH):
                teacher = pt[pl.ds(first + c, R, stride=NC), :]
                s = score[a * R:(a + 1) * R, c * R:(c + 1) * R]
                cells.append((jnp.tanh(s * half_scale + half_bias) - teacher).astype(BF))
            parts.append(jnp.concatenate(cells, axis=1))
        weight = jnp.concatenate(parts, axis=0)
        dI[zb] += jnp.dot(weight, texts, preferred_element_type=F32).reshape(2, R, E)
        dT[columns] += lax.dot_general(
            weight, rows, (((0,), (0,)), ((), ())), preferred_element_type=F32
        ).reshape(NH, R, E)

    def chip_sum(i, rows):
        hh, dx = SPOTS[i]
        return dT[blk(hcol(hh), x + dx, k), rows] + dr[i, rows].astype(F32)

    def arrived(name, rows):
        _, into, i, _ = landing(name)
        return into[i, rows].astype(F32)

    def send(name):
        needs = NEEDS.get(name, ())
        arrive(needs)
        base, rows = split(name)
        kind = base[0]
        value = None
        if kind in "qrk":
            dz, other = SUMS[base]
            value = dI[zz(dz), lcol(other), rows]
        elif kind == "d":
            hh, dx = SPOTS[int(base[1])]
            value = dT[blk(hcol(hh), x + dx, 1 - k), rows]
        elif kind in "uv":
            value = chip_sum(4 * int(base[1]) + X_SPOTS[kind + base[2]], rows)
        elif kind == "f":
            value = chip_sum(4, rows)
        if value is not None:
            for other in needs:
                if other[0] != "d":
                    value = value + arrived(other, rows)
            out, _, i, _ = landing(name)
            out[i, rows] = value.astype(BF)
        copy(name).start()

    before, events = [], {0: []}
    for item in SCHEDULE:
        if not isinstance(item, str):
            events[len(events)] = []
        elif len(events) == 1:
            before.append(item)
        else:
            events[len(events) - 1].append(item)

    lax.fori_loop(0, EARLY, teacher_rows, 0)
    pl.semaphore_wait(barrier, 7)
    done = EARLY
    for n, name in enumerate(before):
        if name != "T":
            send(name)
        elif n + 1 == len(before) or before[n + 1] != "T":
            first, run = done, 1
            while run <= n and before[n - run] == "T":
                run += 1
            done = first + run
            lax.fori_loop(first, done, teacher_rows, 0)

    def step(s, carry):
        for n, (hh, d) in enumerate(TILES):
            names = events[n] if n else ()
            waits = tuple(w for w in IMAGES[d] + TEXTS[hh] if w not in seen)
            if names or waits:

                def event(names=names, waits=waits):
                    for name in names:
                        send(name)
                    arrive(waits)

                pl.when(s == n)(event)
        zb, hb = jnp.int32(0), jnp.int32(0)
        for n, (hh, d) in enumerate(TILES):
            zb = jnp.where(s == n, zz(d), zb)
            hb = jnp.where(s == n, hcol(hh), hb)
        pairs(zb, hb)
        return carry

    lax.fori_loop(0, len(TILES), step, 0)
    for name in events[len(TILES)]:
        send(name)

    whole = pl.ds(0, R)
    unit, mag = unit_rows(txt_ref[...].astype(F32))
    arrive(LAST_TEXT)
    grad = chip_sum(0, whole) + arrived("u01", whole) + arrived("v01", whole) + arrived("f", whole)
    dtxt_ref[...] = unit_grad(half_scale * grad, unit, mag)

    unit, mag = unit_rows(img_ref[...].astype(F32))
    arrive(LAST_IMAGE)
    grad = dI[z, l] + arrived("k3", whole) + arrived("q3", whole) + arrived("r3", whole)
    dimg_ref[...] = unit_grad(half_scale * grad, unit, mag)

    for name in COPIES:
        copy(name).wait_send()


def hand_out(a_ref, b_ref, a_out, b_out):
    a_out[...] = a_ref[...]
    b_out[...] = b_ref[...]


def shards(images, texts, teacher_codes, teacher_scales, student_logit_scale, logit_bias):
    vmem = pl.BlockSpec(memory_space=pltpu.VMEM)
    smem = pl.BlockSpec(memory_space=pltpu.SMEM)
    row = lambda *n: pltpu.VMEM((*n, R, E), BF)
    dma = lambda n: pltpu.SemaphoreType.DMA((n,))
    out = jax.ShapeDtypeStruct((R, E), F32)
    grads = pl.pallas_call(
        kernel,
        out_shape=(out, out),
        in_specs=[vmem, vmem, pl.BlockSpec(memory_space=pl.ANY), vmem, smem, smem],
        out_specs=(vmem, vmem),
        scratch_shapes=[
            pltpu.VMEM((NC * R, NC, R), BF),
            pltpu.VMEM((NC, NC, R), F32),
            pltpu.VMEM((NC * R * NC, R), F32),
            row(NZ, 2),
            row(NC),
            pltpu.VMEM((NZ, 2, R, E), F32),
            pltpu.VMEM((NC, R, E), F32),
            row(12), row(12), row(4), row(4), row(8), row(8), row(8), row(8), row(1), row(1),
            dma(NC), dma(len(COPIES)), dma(len(COPIES)),
        ],
        compiler_params=pltpu.CompilerParams(
            collective_id=0, has_side_effects=True, vmem_limit_bytes=54 * 1024 * 1024
        ),
    )(images, texts, teacher_codes, jnp.swapaxes(teacher_scales, 1, 2), student_logit_scale, logit_bias)
    return pl.pallas_call(hand_out, out_shape=(out, out), in_specs=[vmem] * 2, out_specs=(vmem,) * 2)(*grads)


def solution(mesh):
    in_specs = (
        P(("blk", "tile"), None),
        P(("blk", "tile"), None),
        P("blk", None, "tile"),
        P("blk", None, "tile"),
        P(),
        P(),
    )
    out_specs = (P(("blk", "tile"), None), P(("blk", "tile"), None))
    return jax.shard_map(shards, mesh=mesh, in_specs=in_specs, out_specs=out_specs, check_vma=False)
```

```python
import jax
import jax.numpy as jnp
from jax import lax
from jax.experimental import pallas as pl
from jax.experimental.pallas import tpu as pltpu
from jax.sharding import PartitionSpec as P

EPS = 1e-06
F32 = jnp.float32
BF = jnp.bfloat16
R = 128
E = 512
NZ = 8
NX = 4
NC = 16
NH = 8
PITCH = NC * R + 8
EARLY = 8
PIECES = {"": (0, R), "a": (0, R // 2), "b": (R // 2, R // 2)}

SCHEDULE = (
    "yh", "p0a", "m0b", "xm0", "xp0", "m0a", "p0b", "T", "p1a", "y0", "m1b", "p1b", "m1a", "xp1", "xm1", "T",
    "xm2b", "p3a", "m3b", "xp2a", "c0", "T", "c2", "p2", "y2", "m2", "xp3a", "xm3b", "T", "c5", "p4a", "T",
    "c6", "m4b", "m3a", "p3b", "y1", "c3", "T", "c1", "T", "c4", "p5", "T", "c7", (0, -1), "y3", (1, -1),
    (1, 0), "m5", (2, 1), "q4", (2, -3), "r5", (2, 4), "k2b", "k2a", (2, 3), "q5", "r4", (2, -2), "k1a", "r0b",
    (1, 2), "q0a", "r1a", "d7", "k1b", "d6", "d5", (0, 2), "u10a", "v10b", "k0b", "q1b", (0, 0), "d4", "u11b",
    "k0a", "d2", "r1b", "q1a", "v11a", "d3", "k3", "d1", "u11a", "u00a", "r2a", "v11b", "q2b", "v00b", "r2b",
    "q2a", "v01a", "fa", "u01b", "q3b", "u01a", "r3a", "v01b", "fb", "r3b", "d0", "q3a",
)
NEEDS = {
    "p1a": ("p0a",), "p1b": ("p0b",), "m1a": ("m0a",), "m1b": ("m0b",), "p2": ("y0",), "m2": ("y0",),
    "p3a": ("p1a",), "p3b": ("p1b",), "m3a": ("m1a",), "m3b": ("m1b",), "p4a": ("p3a",), "m4b": ("m3b",),
    "y1": ("m1a", "m1b"), "y2": ("p1a", "p1b"), "p5": ("y2",), "m5": ("y1",), "y3": ("p4a", "m4b"),
    "xp2a": ("xp0",), "xm2b": ("xm0",), "c1": ("xp0",), "c2": ("xm0",), "c3": ("xp2a", "xm2b"), "c4": ("yh",),
    "xp1": ("yh",), "xm1": ("yh",), "c5": ("xp1",), "c6": ("xm1",), "xp3a": ("xp1",), "xm3b": ("xm1",),
    "c7": ("xp3a", "xm3b"), "k3": ("q4", "r4"), "q0a": ("k2a",), "r0b": ("k2b",), "q1a": ("q0a",),
    "r1b": ("r0b",), "k0a": ("q5",), "k0b": ("q5",), "k1a": ("r5",), "k1b": ("r5",), "q2a": ("k0a", "q1a"),
    "q2b": ("k0b", "q1b"), "r2a": ("k1a", "r1a"), "r2b": ("k1b", "r1b"), "q3a": ("q2a",), "q3b": ("q2b",),
    "r3a": ("r2a",), "r3b": ("r2b",), "u10a": ("d7",), "v10b": ("d7",), "u11b": ("d6",), "v11a": ("d5",),
    "u11a": ("d6", "u10a"), "v11b": ("d5", "v10b"), "fa": ("d4", "u11a", "v11a"), "fb": ("d4", "u11b", "v11b"),
    "u00a": ("d3",), "v00b": ("d3",), "u01b": ("d2",), "v01a": ("d1",), "u01a": ("d2", "u00a"),
    "v01b": ("d1", "v00b"),
}
IMAGES = {
    0: ("y0",), 1: ("m0a", "m0b", "m2"), -1: ("p0a", "p0b", "p2"), 2: ("m1a", "m1b", "y1"),
    -2: ("p1a", "p1b", "y2"), 3: ("m3a", "m3b", "m5"), -3: ("p3a", "p3b", "p5"), 4: ("p4a", "m4b", "y3"),
}
TEXTS = (
    ("c0", "c1", "c2", "c3", "xp0", "xm0", "xp2a", "xm2b"),
    ("yh", "xp1", "xm1", "xp3a", "xm3b", "c4", "c5", "c6", "c7"),
)
LAST_TEXT = ("d0", "u01a", "u01b", "v01a", "v01b", "fa", "fb")
LAST_IMAGE = ("k3", "q3a", "q3b", "r3a", "r3b")
SUMS = {
    "q0": (4, 0), "q1": (3, 0), "q2": (2, 0), "q3": (1, 0), "q4": (1, 1), "q5": (3, 1),
    "r0": (4, 0), "r1": (-3, 0), "r2": (-2, 0), "r3": (-1, 0), "r4": (-1, 1), "r5": (-3, 1),
    "g0": (4, 1), "g1": (4, 1), "k0": (2, 1), "k1": (-2, 1), "k2": (4, 1), "k3": (0, 1),
}
SPOTS = ((0, 0), (0, -1), (0, 1), (0, 2), (1, 0), (1, -1), (1, 1), (1, 2))
X_SPOTS = {"u0": 3, "v0": 3, "u1": 2, "v1": 1, "w": 3}
COPIES = tuple(n for n in SCHEDULE if isinstance(n, str) and n != "T")
TILES = tuple(n for n in SCHEDULE if not isinstance(n, str))


def split(name):
    piece = name[-1] if name[-1] in "ab" else ""
    return name[: len(name) - len(piece)], pl.ds(*PIECES[piece])


def unit_rows(values):
    magnitude = jnp.sqrt(jnp.sum(values * values, axis=-1, keepdims=True) + EPS)
    return values / magnitude, magnitude


def unit_grad(grad_unit, unit_vectors, magnitude):
    inner = jnp.sum(unit_vectors * grad_unit, axis=-1, keepdims=True)
    return (grad_unit - unit_vectors * inner) / magnitude


def kernel(
    img_ref, txt_ref, codes_ref, scales_ref, scale_ref, bias_ref,
    dimg_ref, dtxt_ref,
    codes, scb, pt, J, T, dI, dT, zs, zr, ks, kr, ds_, dr, xs, xr, fs, fr, gs, gr, ws, wr,
    codes_sem, ssem, rsem,
):
    bi, ti = lax.axis_index("blk"), lax.axis_index("tile")
    h, x, k = bi // 8, (bi // 2) % NX, bi % 2
    l, z = ti // NZ, ti % NZ

    def blk(hh, xx, kk):
        return hh * 8 + ((xx + 8) % NX) * 2 + kk

    def zz(d):
        return (z + d + 16) % NZ

    def hcol(other):
        return 1 - h if other else h

    def lcol(other):
        return 1 - l if other else l

    up, down = {"tile": l * NZ + zz(1)}, {"tile": l * NZ + zz(-1)}
    ylo = {"tile": (1 - l) * NZ + z}
    yhi = {"blk": blk(1 - h, x, k)}
    right, left = {"blk": blk(h, x + 1, k)}, {"blk": blk(h, x - 1, k)}
    core = {"blk": blk(h, x, 1 - k)}
    across = {"blk": blk(h, x + 2, k)}
    up_ylo, down_ylo = {"tile": (1 - l) * NZ + zz(1)}, {"tile": (1 - l) * NZ + zz(-1)}
    partners = [up, down, ylo, yhi, right, left, core]
    if any(n[0] == "g" for n in COPIES):
        partners += [up_ylo, down_ylo]
    if any(n[0] == "w" or n[:2] == "xx" for n in COPIES):
        partners += [across]

    def codes_copy(r):
        rows = pl.ds(r * R, R)
        return pltpu.make_async_copy(codes_ref.at[rows], codes.at[rows], codes_sem.at[r])

    barrier = pltpu.get_barrier_semaphore()
    for dev in partners:
        pl.semaphore_signal(barrier, inc=1, device_id=dev, device_id_type=pl.DeviceIdType.MESH)
    for r in range(NC):
        codes_copy(r).start()

    def landing(name):
        base, rows = split(name)
        i = int(base[1]) if base[0] in "qrkgduvw" else 0
        if base[0] in "qr":
            return zs, zr, i if base[0] == "q" else 6 + i, rows
        if base[0] == "k":
            return ks, kr, i, rows
        if base[0] == "g":
            return gs, gr, i, rows
        if base[0] == "w":
            return ws, wr, i, rows
        if base[0] == "d":
            return ds_, dr, i, rows
        if base[0] == "f":
            return fs, fr, 0, rows
        return xs, xr, i * 4 + int(base[2]) * 2 + (base[0] == "v"), rows

    def copy(name):
        base, rows = split(name)
        kind = base[0]
        if kind in "pmy" and base != "yh":
            n = int(base[1])
            dz = {"p": (0, -1, 0, -2, -3, -2, -3), "m": (0, 1, 0, 2, 3, 2, 3), "y": (0, 2, -2, 4)}[kind][n]
            spot = J.at[zz(dz), lcol(kind != "y" and n in (2, 5)), rows]
            src, dst, dev = spot, spot, {"p": up, "m": down, "y": ylo}[kind]
            if n == 6:
                dev = up_ylo if kind == "p" else down_ylo
        elif kind in "xyc":
            if base == "yh":
                spot, dev = T.at[bi, rows], yhi
            elif base[:2] == "xx":
                spot, dev = T.at[blk(hcol(base == "xx3"), x, k), rows], across
            elif kind == "c":
                hh, dx = SPOTS[int(base[1])]
                spot, dev = T.at[blk(hcol(hh), x + dx, k), rows], core
            else:
                n, sign = int(base[2]), 1 if base[1] == "p" else -1
                spot = T.at[blk(hcol(n % 2), x - sign if n >= 2 else x, k), rows]
                dev = right if sign == 1 else left
            src, dst = spot, spot
        else:
            out, into, i, rows = landing(name)
            src, dst = out.at[i, rows], into.at[i, rows]
            dev = {"g": down_ylo if i else up_ylo, "w": across, "q": up, "r": down, "k": ylo, "d": core, "u": right, "v": left, "f": yhi}[kind]
        i = COPIES.index(name)
        return pltpu.make_async_remote_copy(
            src_ref=src, dst_ref=dst, send_sem=ssem.at[i], recv_sem=rsem.at[i], device_id=dev,
            device_id_type=pl.DeviceIdType.MESH,
        )

    seen = set()

    def arrive(names):
        for name in names:
            if name not in seen:
                seen.add(name)
                copy(name).wait_recv()

    img_unit, _ = unit_rows(img_ref[...].astype(F32))
    J[z, l] = img_unit.astype(BF)
    txt_unit, _ = unit_rows(txt_ref[...].astype(F32))
    T[bi] = txt_unit.astype(BF)

    eye = lax.broadcasted_iota(jnp.int32, (NC, NC), 0) == lax.broadcasted_iota(jnp.int32, (NC, NC), 1)
    for r in range(NC):
        row = jnp.broadcast_to(scales_ref[r], (NC, NC))
        column = jnp.sum(jnp.where(eye, row, 0.0), axis=-1, keepdims=True)
        scb[r] = jnp.broadcast_to(0.5 * column, (NC, R))

    def teacher_rows(r, carry):
        codes_copy(r).wait()
        sc = scb[r]
        dT[r] = jnp.zeros((R, E), F32)
        dI[r // 2, r % 2] = jnp.zeros((R, E), F32)

        def some(g, inner):
            for u in range(16):
                i = r * R + g * 16 + u
                pt[pl.ds(i, NC, stride=PITCH), :] = jnp.tanh(codes[i].astype(F32) * sc)
            return inner

        return lax.fori_loop(0, R // 16, some, carry)

    half_scale = 0.5 * scale_ref[0]
    half_bias = 0.5 * bias_ref[0]

    def pairs(zb, hb, count):
        rows = J[zb].reshape(2 * R, E)
        columns = pl.ds(hb * NH, count)
        texts = T[columns].reshape(count * R, E)
        score = lax.dot_general(rows, texts, (((1,), (1,)), ((), ())), preferred_element_type=F32)
        parts = []
        for a in range(2):
            first = hb * (NH * PITCH) + (a * NZ + zb) * R
            cells = []
            for c in range(count):
                teacher = pt[pl.ds(pl.multiple_of(first + c * PITCH, 8), R), :]
                s = score[a * R:(a + 1) * R, c * R:(c + 1) * R]
                cells.append((jnp.tanh(s * half_scale + half_bias) - teacher).astype(BF))
            parts.append(jnp.concatenate(cells, axis=1))
        weight = jnp.concatenate(parts, axis=0)
        part = jnp.dot(weight, texts, preferred_element_type=F32).reshape(2, R, E)
        dI[zb] = part if count == NC else dI[zb] + part
        dT[columns] += lax.dot_general(
            weight, rows, (((0,), (0,)), ((), ())), preferred_element_type=F32
        ).reshape(count, R, E)

    def chip_sum(i, rows):
        hh, dx = SPOTS[i]
        return dT[blk(hcol(hh), x + dx, k), rows] + dr[i, rows].astype(F32)

    def arrived(name, rows):
        _, into, i, _ = landing(name)
        return into[i, rows].astype(F32)

    def send(name):
        needs = NEEDS.get(name, ())
        arrive(needs)
        base, rows = split(name)
        kind = base[0]
        value = None
        if kind in "qrkg":
            dz, other = SUMS[base]
            value = dI[zz(dz), lcol(other), rows]
        elif kind == "d":
            hh, dx = SPOTS[int(base[1])]
            value = dT[blk(hcol(hh), x + dx, 1 - k), rows]
        elif kind in "uvw":
            value = chip_sum(4 * int(base[1]) + X_SPOTS[kind + base[2:]], rows)
        elif kind == "f":
            value = chip_sum(4, rows)
        if value is not None:
            for other in needs:
                if other[0] != "d":
                    value = value + arrived(other, rows)
            out, _, i, _ = landing(name)
            out[i, rows] = value.astype(BF)
        copy(name).start()

    before, events = [], {0: []}
    for item in SCHEDULE:
        if not isinstance(item, str):
            events[len(events)] = []
        elif len(events) == 1:
            before.append(item)
        else:
            events[len(events) - 1].append(item)

    lax.fori_loop(0, EARLY, teacher_rows, 0)
    pl.semaphore_wait(barrier, len(partners))
    done = EARLY
    for n, name in enumerate(before):
        if name != "T":
            send(name)
        elif n + 1 == len(before) or before[n + 1] != "T":
            first, run = done, 1
            while run <= n and before[n - run] == "T":
                run += 1
            done = first + run
            lax.fori_loop(first, done, teacher_rows, 0)

    def step(s, carry):
        for n, (hh, d) in enumerate(TILES):
            names = events[n] if n else ()
            texts = TEXTS[hh] if hh < 2 else TEXTS[0] + TEXTS[1]
            waits = tuple(w for w in IMAGES[d] + texts if w not in seen)
            if names or waits:

                def event(names=names, waits=waits):
                    for name in names:
                        send(name)
                    arrive(waits)

                pl.when(s == n)(event)
        zb, hb, full = jnp.int32(0), jnp.int32(0), jnp.int32(0)
        for n, (hh, d) in enumerate(TILES):
            zb = jnp.where(s == n, zz(d), zb)
            if hh < 2:
                hb = jnp.where(s == n, hcol(hh), hb)
            else:
                full = jnp.where(s == n, 1, full)
        pl.when(full == 0)(lambda: pairs(zb, hb, NH))
        pl.when(full == 1)(lambda: pairs(zb, 0, NC))
        return carry

    lax.fori_loop(0, len(TILES), step, 0)
    for name in events[len(TILES)]:
        send(name)

    whole = pl.ds(0, R)
    unit, mag = unit_rows(txt_ref[...].astype(F32))
    arrive(LAST_TEXT)
    grad = chip_sum(0, whole)
    for name in sorted({split(n)[0] for n in LAST_TEXT if n[0] != "d"}):
        grad = grad + arrived(name, whole)
    dtxt_ref[...] = unit_grad(half_scale * grad, unit, mag)

    unit, mag = unit_rows(img_ref[...].astype(F32))
    arrive(LAST_IMAGE)
    grad = dI[z, l] + arrived("k3", whole) + arrived("q3", whole) + arrived("r3", whole)
    dimg_ref[...] = unit_grad(half_scale * grad, unit, mag)

    for name in COPIES:
        copy(name).wait_send()


def shards(images, texts, teacher_codes, teacher_scales, student_logit_scale, logit_bias):
    vmem = pl.BlockSpec(memory_space=pltpu.VMEM)
    smem = pl.BlockSpec(memory_space=pltpu.SMEM)
    row = lambda *n: pltpu.VMEM((*n, R, E), BF)
    dma = lambda n: pltpu.SemaphoreType.DMA((n,))
    out = pltpu.VMEM((R, E), F32)
    return pl.pallas_call(
        kernel,
        out_shape=(out, out),
        in_specs=[vmem, vmem, pl.BlockSpec(memory_space=pl.ANY), vmem, smem, smem],
        out_specs=(vmem, vmem),
        scratch_shapes=[
            pltpu.VMEM((NC * R, NC, R), BF),
            pltpu.VMEM((NC, NC, R), F32),
            pltpu.VMEM((NC * PITCH, R), F32),
            row(NZ, 2),
            row(NC),
            pltpu.VMEM((NZ, 2, R, E), F32),
            pltpu.VMEM((NC, R, E), F32),
            row(12), row(12), row(4), row(4), row(8), row(8), row(8), row(8), row(1), row(1), row(2), row(2), row(2), row(2),
            dma(NC), dma(len(COPIES)), dma(len(COPIES)),
        ],
        compiler_params=pltpu.CompilerParams(
            collective_id=0, has_side_effects=True, vmem_limit_bytes=54 * 1024 * 1024
        ),
    )(images, texts, teacher_codes, jnp.swapaxes(teacher_scales, 1, 2), student_logit_scale, logit_bias)


def solution(mesh):
    in_specs = (
        P(("blk", "tile"), None),
        P(("blk", "tile"), None),
        P("blk", None, "tile"),
        P("blk", None, "tile"),
        P(),
        P(),
    )
    out_specs = (P(("blk", "tile"), None), P(("blk", "tile"), None))
    return jax.shard_map(shards, mesh=mesh, in_specs=in_specs, out_specs=out_specs, check_vma=False)
```

```python
import jax
import jax.numpy as jnp
from jax import lax
from jax.experimental import pallas as pl
from jax.experimental.pallas import tpu as pltpu
from jax.sharding import PartitionSpec as P

EPS = 1e-06
F32 = jnp.float32
BF = jnp.bfloat16
R = 128
E = 512
NZ = 8
NX = 4
NC = 16
NH = 8
PITCH = NC * R + 8
PIECES = {"": (0, R), "a": (0, R // 2), "b": (R // 2, R // 2)}

SCHEDULE = (
    "yh", "p0a", "m0b", "xm0", "xp0", "m0a", "p0b", "T", "T", "p1a", "y0", "m1b", "p1b", "m1a", "xp1", "xm1",
    "T", "T", "xm2b", "p3a", "m3b", "xp2a", "c0", "T", "T", "c2", "p2", "y2", "m2", "xp3a", "xm3b", "T", "T",
    "c5", "p4a", "T", "T", "c6", "m4b", "m3a", "p3b", "y1", "c3", "T", "T", "c1", "T", "T", "c4", "p5", "T",
    "T", "c7", (0, -1), "y3", (1, -1), (1, 0), "m5", (2, 1), "q4", (2, -3), "r5", (2, 4), "k2b", "k2a", (2, 3),
    "q5", "r4", (2, -2), "k1a", "r0b", (1, 2), "q0a", "r1a", "d7", "k1b", "d6", "d5", (0, 2), "u10a", "v10b",
    "k0b", "q1b", (0, 0), "d4", "u11b", "k0a", "d2", "r1b", "q1a", "v11a", "d3", "k3", "d1", "u11a", "u00a",
    "r2a", "v11b", "q2b", "v00b", "r2b", "q2a", "v01a", "fa", "u01b", "q3b", "u01a", "r3a", "v01b", "fb", "r3b",
    "d0", "q3a",
)
NEEDS = {
    "p1a": ("p0a",), "p1b": ("p0b",), "m1a": ("m0a",), "m1b": ("m0b",), "p2": ("y0",), "m2": ("y0",),
    "p3a": ("p1a",), "p3b": ("p1b",), "m3a": ("m1a",), "m3b": ("m1b",), "p4a": ("p3a",), "m4b": ("m3b",),
    "y1": ("m1a", "m1b"), "y2": ("p1a", "p1b"), "p5": ("y2",), "m5": ("y1",), "y3": ("p4a", "m4b"),
    "xp2a": ("xp0",), "xm2b": ("xm0",), "c1": ("xp0",), "c2": ("xm0",), "c3": ("xp2a", "xm2b"), "c4": ("yh",),
    "xp1": ("yh",), "xm1": ("yh",), "c5": ("xp1",), "c6": ("xm1",), "xp3a": ("xp1",), "xm3b": ("xm1",),
    "c7": ("xp3a", "xm3b"), "k3": ("q4", "r4"), "q0a": ("k2a",), "r0b": ("k2b",), "q1a": ("q0a",),
    "r1b": ("r0b",), "k0a": ("q5",), "k0b": ("q5",), "k1a": ("r5",), "k1b": ("r5",), "q2a": ("k0a", "q1a"),
    "q2b": ("k0b", "q1b"), "r2a": ("k1a", "r1a"), "r2b": ("k1b", "r1b"), "q3a": ("q2a",), "q3b": ("q2b",),
    "r3a": ("r2a",), "r3b": ("r2b",), "u10a": ("d7",), "v10b": ("d7",), "u11b": ("d6",), "v11a": ("d5",),
    "u11a": ("d6", "u10a"), "v11b": ("d5", "v10b"), "fa": ("d4", "u11a", "v11a"), "fb": ("d4", "u11b", "v11b"),
    "u00a": ("d3",), "v00b": ("d3",), "u01b": ("d2",), "v01a": ("d1",), "u01a": ("d2", "u00a"),
    "v01b": ("d1", "v00b"),
}
IMAGES = {
    0: ("y0",), 1: ("m0a", "m0b", "m2"), -1: ("p0a", "p0b", "p2"), 2: ("m1a", "m1b", "y1"),
    -2: ("p1a", "p1b", "y2"), 3: ("m3a", "m3b", "m5"), -3: ("p3a", "p3b", "p5"), 4: ("p4a", "m4b", "y3"),
}
TEXTS = (
    ("c0", "c1", "c2", "c3", "xp0", "xm0", "xp2a", "xm2b"),
    ("yh", "xp1", "xm1", "xp3a", "xm3b", "c4", "c5", "c6", "c7"),
)
LAST_TEXT = ("d0", "u01a", "u01b", "v01a", "v01b", "fa", "fb")
LAST_IMAGE = ("k3", "q3a", "q3b", "r3a", "r3b")
SUMS = {
    "q0": (4, 0), "q1": (3, 0), "q2": (2, 0), "q3": (1, 0), "q4": (1, 1), "q5": (3, 1),
    "r0": (4, 0), "r1": (-3, 0), "r2": (-2, 0), "r3": (-1, 0), "r4": (-1, 1), "r5": (-3, 1),
    "k0": (2, 1), "k1": (-2, 1), "k2": (4, 1), "k3": (0, 1),
}
SPOTS = ((0, 0), (0, -1), (0, 1), (0, 2), (1, 0), (1, -1), (1, 1), (1, 2))
X_SPOTS = {"u0": 3, "v0": 3, "u1": 2, "v1": 1}
COPIES = tuple(n for n in SCHEDULE if isinstance(n, str) and n != "T")
TILES = tuple(n for n in SCHEDULE if not isinstance(n, str))


def split(name):
    piece = name[-1] if name[-1] in "ab" else ""
    return name[: len(name) - len(piece)], pl.ds(*PIECES[piece])


def unit_rows(values):
    magnitude = jnp.sqrt(jnp.sum(values * values, axis=-1, keepdims=True) + EPS)
    return values / magnitude, magnitude


def unit_grad(grad_unit, unit_vectors, magnitude):
    inner = jnp.sum(unit_vectors * grad_unit, axis=-1, keepdims=True)
    return (grad_unit - unit_vectors * inner) / magnitude


def kernel(
    img_hbm, txt_hbm, codes_ref, scales_ref, scale_ref, bias_ref,
    dimg_ref, dtxt_ref,
    codes, scb, pt, J, T, dI, dT, zs, zr, ks, kr, ds_, dr, xs, xr, fs, fr,
    img_ref, txt_ref, in_sem,
    codes_sem, ssem, rsem,
):
    bi, ti = lax.axis_index("blk"), lax.axis_index("tile")
    h, x, k = bi // 8, (bi // 2) % NX, bi % 2
    l, z = ti // NZ, ti % NZ

    def blk(hh, xx, kk):
        return hh * 8 + ((xx + 8) % NX) * 2 + kk

    def zz(d):
        return (z + d + 16) % NZ

    def hcol(other):
        return 1 - h if other else h

    def lcol(other):
        return 1 - l if other else l

    up, down = {"tile": l * NZ + zz(1)}, {"tile": l * NZ + zz(-1)}
    ylo = {"tile": (1 - l) * NZ + z}
    yhi = {"blk": blk(1 - h, x, k)}
    right, left = {"blk": blk(h, x + 1, k)}, {"blk": blk(h, x - 1, k)}
    core = {"blk": blk(h, x, 1 - k)}
    partners = (up, down, ylo, yhi, right, left, core)

    def codes_copy(r):
        rows = pl.ds(r * R, R)
        return pltpu.make_async_copy(codes_ref.at[rows], codes.at[rows], codes_sem.at[r])

    inputs = [
        pltpu.make_async_copy(src, dst, in_sem.at[n])
        for n, (src, dst) in enumerate(((img_hbm, img_ref), (txt_hbm, txt_ref)))
    ]
    for c in inputs:
        c.start()
    barrier = pltpu.get_barrier_semaphore()
    for dev in partners:
        pl.semaphore_signal(barrier, inc=1, device_id=dev, device_id_type=pl.DeviceIdType.MESH)

    def landing(name):
        base, rows = split(name)
        i = int(base[1]) if base[0] in "qrkduv" else 0
        if base[0] in "qr":
            return zs, zr, i if base[0] == "q" else 6 + i, rows
        if base[0] == "k":
            return ks, kr, i, rows
        if base[0] == "d":
            return ds_, dr, i, rows
        if base[0] == "f":
            return fs, fr, 0, rows
        return xs, xr, i * 4 + int(base[2]) * 2 + (base[0] == "v"), rows

    def copy(name):
        base, rows = split(name)
        kind = base[0]
        if kind in "pmy" and base != "yh":
            n = int(base[1])
            dz = {"p": (0, -1, 0, -2, -3, -2), "m": (0, 1, 0, 2, 3, 2), "y": (0, 2, -2, 4)}[kind][n]
            spot = J.at[zz(dz), lcol(kind != "y" and n in (2, 5)), rows]
            src, dst, dev = spot, spot, {"p": up, "m": down, "y": ylo}[kind]
        elif kind in "xyc":
            if base == "yh":
                spot, dev = T.at[bi, rows], yhi
            elif kind == "c":
                hh, dx = SPOTS[int(base[1])]
                spot, dev = T.at[blk(hcol(hh), x + dx, k), rows], core
            else:
                n, sign = int(base[2]), 1 if base[1] == "p" else -1
                spot = T.at[blk(hcol(n % 2), x - sign if n >= 2 else x, k), rows]
                dev = right if sign == 1 else left
            src, dst = spot, spot
        else:
            out, into, i, rows = landing(name)
            src, dst = out.at[i, rows], into.at[i, rows]
            dev = {"q": up, "r": down, "k": ylo, "d": core, "u": right, "v": left, "f": yhi}[kind]
        i = COPIES.index(name)
        return pltpu.make_async_remote_copy(
            src_ref=src, dst_ref=dst, send_sem=ssem.at[i], recv_sem=rsem.at[i], device_id=dev,
            device_id_type=pl.DeviceIdType.MESH,
        )

    seen = set()

    def arrive(names):
        for name in names:
            if name not in seen:
                seen.add(name)
                copy(name).wait_recv()

    for c in inputs:
        c.wait()
    for r in range(NC):
        codes_copy(r).start()
    img_unit, _ = unit_rows(img_ref[...].astype(F32))
    J[z, l] = img_unit.astype(BF)
    txt_unit, _ = unit_rows(txt_ref[...].astype(F32))
    T[bi] = txt_unit.astype(BF)

    def teacher_scales():
        eye = lax.broadcasted_iota(jnp.int32, (NC, NC), 0) == lax.broadcasted_iota(jnp.int32, (NC, NC), 1)
        for r in range(NC):
            row = jnp.broadcast_to(scales_ref[r], (NC, NC))
            column = jnp.sum(jnp.where(eye, row, 0.0), axis=-1, keepdims=True)
            scb[r] = jnp.broadcast_to(0.5 * column, (NC, R))

    def teacher_rows(r, carry):
        codes_copy(r).wait()
        sc = scb[r]
        dT[r] = jnp.zeros((R, E), F32)
        dI[r // 2, r % 2] = jnp.zeros((R, E), F32)

        def some(g, inner):
            for u in range(16):
                i = r * R + g * 16 + u
                pt[pl.ds(i, NC, stride=PITCH), :] = jnp.tanh(codes[i].astype(F32) * sc)
            return inner

        return lax.fori_loop(0, R // 16, some, carry)

    half_scale = 0.5 * scale_ref[0]
    half_bias = 0.5 * bias_ref[0]

    def pairs(zb, hb, count):
        rows = J[zb].reshape(2 * R, E)
        columns = pl.ds(hb * NH, count)
        texts = T[columns].reshape(count * R, E)
        score = lax.dot_general(rows, texts, (((1,), (1,)), ((), ())), preferred_element_type=F32)
        parts = []
        for a in range(2):
            first = hb * (NH * PITCH) + (a * NZ + zb) * R
            cells = []
            for c in range(count):
                teacher = pt[pl.ds(pl.multiple_of(first + c * PITCH, 8), R), :]
                s = score[a * R:(a + 1) * R, c * R:(c + 1) * R]
                cells.append((jnp.tanh(s * half_scale + half_bias) - teacher).astype(BF))
            parts.append(jnp.concatenate(cells, axis=1))
        weight = jnp.concatenate(parts, axis=0)
        part = jnp.dot(weight, texts, preferred_element_type=F32).reshape(2, R, E)
        dI[zb] = part if count == NC else dI[zb] + part
        dT[columns] += lax.dot_general(
            weight, rows, (((0,), (0,)), ((), ())), preferred_element_type=F32
        ).reshape(count, R, E)

    def chip_sum(i, rows):
        hh, dx = SPOTS[i]
        return dT[blk(hcol(hh), x + dx, k), rows] + dr[i, rows].astype(F32)

    def arrived(name, rows):
        _, into, i, _ = landing(name)
        return into[i, rows].astype(F32)

    def send(name):
        needs = NEEDS.get(name, ())
        arrive(needs)
        base, rows = split(name)
        kind = base[0]
        value = None
        if kind in "qrk":
            dz, other = SUMS[base]
            value = dI[zz(dz), lcol(other), rows]
        elif kind == "d":
            hh, dx = SPOTS[int(base[1])]
            value = dT[blk(hcol(hh), x + dx, 1 - k), rows]
        elif kind in "uv":
            value = chip_sum(4 * int(base[1]) + X_SPOTS[kind + base[2]], rows)
        elif kind == "f":
            value = chip_sum(4, rows)
        if value is not None:
            for other in needs:
                if other[0] != "d":
                    value = value + arrived(other, rows)
            out, _, i, _ = landing(name)
            out[i, rows] = value.astype(BF)
        copy(name).start()

    before, events = [], {0: []}
    for item in SCHEDULE:
        if not isinstance(item, str):
            events[len(events)] = []
        elif len(events) == 1:
            before.append(item)
        else:
            events[len(events) - 1].append(item)

    pl.semaphore_wait(barrier, len(partners))
    done = 0
    for n, name in enumerate(before):
        if name != "T":
            send(name)
        elif n + 1 == len(before) or before[n + 1] != "T":
            first, run = done, 1
            while run <= n and before[n - run] == "T":
                run += 1
            done = first + run
            if first == 0:
                teacher_scales()
            lax.fori_loop(first, done, teacher_rows, 0)

    def step(s, carry):
        for n, (hh, d) in enumerate(TILES):
            names = events[n] if n else ()
            texts = TEXTS[hh] if hh < 2 else TEXTS[0] + TEXTS[1]
            waits = tuple(w for w in IMAGES[d] + texts if w not in seen)
            if names or waits:

                def event(names=names, waits=waits):
                    for name in names:
                        send(name)
                    arrive(waits)

                pl.when(s == n)(event)
        zb, hb, full = jnp.int32(0), jnp.int32(0), jnp.int32(0)
        for n, (hh, d) in enumerate(TILES):
            zb = jnp.where(s == n, zz(d), zb)
            if hh < 2:
                hb = jnp.where(s == n, hcol(hh), hb)
            else:
                full = jnp.where(s == n, 1, full)
        pl.when(full == 0)(lambda: pairs(zb, hb, NH))
        pl.when(full == 1)(lambda: pairs(zb, 0, NC))
        return carry

    lax.fori_loop(0, len(TILES), step, 0)
    for name in events[len(TILES)]:
        send(name)

    late = COPIES[-16:]
    for name in COPIES:
        if name not in late:
            copy(name).wait_send()

    whole = pl.ds(0, R)
    unit, mag = unit_rows(txt_ref[...].astype(F32))
    arrive(LAST_TEXT)
    grad = chip_sum(0, whole)
    for name in sorted({split(n)[0] for n in LAST_TEXT if n[0] != "d"}):
        grad = grad + arrived(name, whole)
    dtxt_ref[...] = unit_grad(half_scale * grad, unit, mag)

    unit, mag = unit_rows(img_ref[...].astype(F32))
    arrive(LAST_IMAGE)
    grad = dI[z, l] + arrived("k3", whole) + arrived("q3", whole) + arrived("r3", whole)
    dimg_ref[...] = unit_grad(half_scale * grad, unit, mag)

    for name in late:
        copy(name).wait_send()


def shards(images, texts, teacher_codes, teacher_scales, student_logit_scale, logit_bias):
    vmem = pl.BlockSpec(memory_space=pltpu.VMEM)
    smem = pl.BlockSpec(memory_space=pltpu.SMEM)
    hbm = pl.BlockSpec(memory_space=pl.ANY)
    row = lambda *n: pltpu.VMEM((*n, R, E), BF)
    dma = lambda n: pltpu.SemaphoreType.DMA((n,))
    out = pltpu.VMEM((R, E), F32)
    return pl.pallas_call(
        kernel,
        out_shape=(out, out),
        in_specs=[hbm, hbm, hbm, vmem, smem, smem],
        out_specs=(vmem, vmem),
        scratch_shapes=[
            pltpu.VMEM((NC * R, NC, R), BF),
            pltpu.VMEM((NC, NC, R), F32),
            pltpu.VMEM((NC * PITCH, R), F32),
            row(NZ, 2),
            row(NC),
            pltpu.VMEM((NZ, 2, R, E), F32),
            pltpu.VMEM((NC, R, E), F32),
            row(12), row(12), row(4), row(4), row(8), row(8), row(8), row(8), row(1), row(1),
            row(), row(), dma(2),
            dma(NC), dma(len(COPIES)), dma(len(COPIES)),
        ],
        compiler_params=pltpu.CompilerParams(
            collective_id=0, has_side_effects=True, vmem_limit_bytes=54 * 1024 * 1024
        ),
    )(images, texts, teacher_codes, jnp.swapaxes(teacher_scales, 1, 2), student_logit_scale, logit_bias)


def solution(mesh):
    in_specs = (
        P(("blk", "tile"), None),
        P(("blk", "tile"), None),
        P("blk", None, "tile"),
        P("blk", None, "tile"),
        P(),
        P(),
    )
    out_specs = (P(("blk", "tile"), None), P(("blk", "tile"), None))
    return jax.shard_map(shards, mesh=mesh, in_specs=in_specs, out_specs=out_specs, check_vma=False)
```

```python
import jax
import jax.numpy as jnp
from jax import lax
from jax.experimental import pallas as pl
from jax.experimental.pallas import tpu as pltpu
from jax.sharding import PartitionSpec as P

EPS = 1e-06
F32 = jnp.float32
BF = jnp.bfloat16
R = 128
E = 512
NZ = 8
NX = 4
NC = 16
NH = 8
PITCH = NC * R + 8
PIECES = {"": (0, R), "a": (0, R // 2), "b": (R // 2, R // 2)}

SCHEDULE = (
    "yh", "p0a", "m0b", "xm0", "xp0", "m0a", "p0b", "T", "T", "p1a", "y0", "m1b", "p1b", "m1a", "xp1", "xm1",
    "T", "T", "xm2b", "p3a", "m3b", "xp2a", "c0", "T", "T", "c2", "p2", "y2", "m2", "xp3a", "xm3b", "T", "T",
    "c5", "p4a", "T", "T", "c6", "m4b", "m3a", "p3b", "y1", "c3", "T", "T", "c1", "T", "T", "c4", "p5", "T",
    "T", "c7", (0, -1), "y3", (1, -1), (1, 0), "m5", (2, 1), "q4", (2, -3), "r5", (2, 4), "k2b", "k2a", (2, 3),
    "q5", "r4", (2, -2), "k1a", "r0b", (1, 2), "q0a", "r1a", "d7", "k1b", "d6", "d5", (0, 2), "u10a", "v10b",
    "k0b", "q1b", (0, 0), "d4", "u11b", "k0a", "d2", "r1b", "q1a", "v11a", "d3", "k3", "d1", "u11a", "u00a",
    "r2a", "v11b", "q2b", "v00b", "r2b", "q2a", "v01a", "fa", "u01b", "q3b", "u01a", "r3a", "v01b", "fb", "r3b",
    "d0", "q3a",
)
NEEDS = {
    "p1a": ("p0a",), "p1b": ("p0b",), "m1a": ("m0a",), "m1b": ("m0b",), "p2": ("y0",), "m2": ("y0",),
    "p3a": ("p1a",), "p3b": ("p1b",), "m3a": ("m1a",), "m3b": ("m1b",), "p4a": ("p3a",), "m4b": ("m3b",),
    "y1": ("m1a", "m1b"), "y2": ("p1a", "p1b"), "p5": ("y2",), "m5": ("y1",), "y3": ("p4a", "m4b"),
    "xp2a": ("xp0",), "xm2b": ("xm0",), "c1": ("xp0",), "c2": ("xm0",), "c3": ("xp2a", "xm2b"), "c4": ("yh",),
    "xp1": ("yh",), "xm1": ("yh",), "c5": ("xp1",), "c6": ("xm1",), "xp3a": ("xp1",), "xm3b": ("xm1",),
    "c7": ("xp3a", "xm3b"), "k3": ("q4", "r4"), "q0a": ("k2a",), "r0b": ("k2b",), "q1a": ("q0a",),
    "r1b": ("r0b",), "k0a": ("q5",), "k0b": ("q5",), "k1a": ("r5",), "k1b": ("r5",), "q2a": ("k0a", "q1a"),
    "q2b": ("k0b", "q1b"), "r2a": ("k1a", "r1a"), "r2b": ("k1b", "r1b"), "q3a": ("q2a",), "q3b": ("q2b",),
    "r3a": ("r2a",), "r3b": ("r2b",), "u10a": ("d7",), "v10b": ("d7",), "u11b": ("d6",), "v11a": ("d5",),
    "u11a": ("d6", "u10a"), "v11b": ("d5", "v10b"), "fa": ("d4", "u11a", "v11a"), "fb": ("d4", "u11b", "v11b"),
    "u00a": ("d3",), "v00b": ("d3",), "u01b": ("d2",), "v01a": ("d1",), "u01a": ("d2", "u00a"),
    "v01b": ("d1", "v00b"),
}
IMAGES = {
    0: ("y0",), 1: ("m0a", "m0b", "m2"), -1: ("p0a", "p0b", "p2"), 2: ("m1a", "m1b", "y1"),
    -2: ("p1a", "p1b", "y2"), 3: ("m3a", "m3b", "m5"), -3: ("p3a", "p3b", "p5"), 4: ("p4a", "m4b", "y3"),
}
TEXTS = (
    ("c0", "c1", "c2", "c3", "xp0", "xm0", "xp2a", "xm2b"),
    ("yh", "xp1", "xm1", "xp3a", "xm3b", "c4", "c5", "c6", "c7"),
)
LAST_TEXT = ("d0", "u01a", "u01b", "v01a", "v01b", "fa", "fb")
LAST_IMAGE = ("k3", "q3a", "q3b", "r3a", "r3b")
SUMS = {
    "q0": (4, 0), "q1": (3, 0), "q2": (2, 0), "q3": (1, 0), "q4": (1, 1), "q5": (3, 1),
    "r0": (4, 0), "r1": (-3, 0), "r2": (-2, 0), "r3": (-1, 0), "r4": (-1, 1), "r5": (-3, 1),
    "k0": (2, 1), "k1": (-2, 1), "k2": (4, 1), "k3": (0, 1),
}
SPOTS = ((0, 0), (0, -1), (0, 1), (0, 2), (1, 0), (1, -1), (1, 1), (1, 2))
X_SPOTS = {"u0": 3, "v0": 3, "u1": 2, "v1": 1}
COPIES = tuple(n for n in SCHEDULE if isinstance(n, str) and n != "T")
TILES = tuple(n for n in SCHEDULE if not isinstance(n, str))


def split(name):
    piece = name[-1] if name[-1] in "ab" else ""
    return name[: len(name) - len(piece)], pl.ds(*PIECES[piece])


def unit_rows(values):
    magnitude = jnp.sqrt(jnp.sum(values * values, axis=-1, keepdims=True) + EPS)
    return values / magnitude, magnitude


def unit_grad(grad_unit, unit_vectors, magnitude):
    inner = jnp.sum(unit_vectors * grad_unit, axis=-1, keepdims=True)
    return (grad_unit - unit_vectors * inner) / magnitude


def kernel(
    img_hbm, txt_hbm, codes_ref, scales_ref, scale_ref, bias_ref,
    dimg_ref, dtxt_ref,
    codes, scb, pt, J, T, dI, dT, zs, zr, ks, kr, ds_, dr, xs, xr, fs, fr,
    img_ref, txt_ref, in_sem,
    codes_sem, ssem, rsem,
):
    bi, ti = lax.axis_index("blk"), lax.axis_index("tile")
    h, x, k = bi // 8, (bi // 2) % NX, bi % 2
    l, z = ti // NZ, ti % NZ

    def blk(hh, xx, kk):
        return hh * 8 + ((xx + 8) % NX) * 2 + kk

    def zz(d):
        return (z + d + 16) % NZ

    def hcol(other):
        return 1 - h if other else h

    def lcol(other):
        return 1 - l if other else l

    up, down = {"tile": l * NZ + zz(1)}, {"tile": l * NZ + zz(-1)}
    ylo = {"tile": (1 - l) * NZ + z}
    yhi = {"blk": blk(1 - h, x, k)}
    right, left = {"blk": blk(h, x + 1, k)}, {"blk": blk(h, x - 1, k)}
    core = {"blk": blk(h, x, 1 - k)}
    partners = (up, down, ylo, yhi, right, left, core)

    def codes_copy(r):
        rows = pl.ds(r * R, R)
        return pltpu.make_async_copy(codes_ref.at[rows], codes.at[rows], codes_sem.at[r])

    inputs = [
        pltpu.make_async_copy(src, dst, in_sem.at[n])
        for n, (src, dst) in enumerate(((img_hbm, img_ref), (txt_hbm, txt_ref)))
    ]
    for c in inputs:
        c.start()
    barrier = pltpu.get_barrier_semaphore()
    for dev in partners:
        pl.semaphore_signal(barrier, inc=1, device_id=dev, device_id_type=pl.DeviceIdType.MESH)

    def landing(name):
        base, rows = split(name)
        i = int(base[1]) if base[0] in "qrkduv" else 0
        if base[0] in "qr":
            return zs, zr, i if base[0] == "q" else 6 + i, rows
        if base[0] == "k":
            return ks, kr, i, rows
        if base[0] == "d":
            return ds_, dr, i, rows
        if base[0] == "f":
            return fs, fr, 0, rows
        return xs, xr, i * 4 + int(base[2]) * 2 + (base[0] == "v"), rows

    def copy(name):
        base, rows = split(name)
        kind = base[0]
        if kind in "pmy" and base != "yh":
            n = int(base[1])
            dz = {"p": (0, -1, 0, -2, -3, -2), "m": (0, 1, 0, 2, 3, 2), "y": (0, 2, -2, 4)}[kind][n]
            spot = J.at[zz(dz), lcol(kind != "y" and n in (2, 5)), rows]
            src, dst, dev = spot, spot, {"p": up, "m": down, "y": ylo}[kind]
        elif kind in "xyc":
            if base == "yh":
                spot, dev = T.at[bi, rows], yhi
            elif kind == "c":
                hh, dx = SPOTS[int(base[1])]
                spot, dev = T.at[blk(hcol(hh), x + dx, k), rows], core
            else:
                n, sign = int(base[2]), 1 if base[1] == "p" else -1
                spot = T.at[blk(hcol(n % 2), x - sign if n >= 2 else x, k), rows]
                dev = right if sign == 1 else left
            src, dst = spot, spot
        else:
            out, into, i, rows = landing(name)
            src, dst = out.at[i, rows], into.at[i, rows]
            dev = {"q": up, "r": down, "k": ylo, "d": core, "u": right, "v": left, "f": yhi}[kind]
        i = COPIES.index(name)
        return pltpu.make_async_remote_copy(
            src_ref=src, dst_ref=dst, send_sem=ssem.at[i], recv_sem=rsem.at[i], device_id=dev,
            device_id_type=pl.DeviceIdType.MESH,
        )

    seen = set()

    def arrive(names):
        for name in names:
            if name not in seen:
                seen.add(name)
                copy(name).wait_recv()

    for c in inputs:
        c.wait()
    for r in range(NC):
        codes_copy(r).start()
    img_unit, _ = unit_rows(img_ref[...].astype(F32))
    J[z, l] = img_unit.astype(BF)
    txt_unit, _ = unit_rows(txt_ref[...].astype(F32))
    T[bi] = txt_unit.astype(BF)

    def teacher_scales():
        eye = lax.broadcasted_iota(jnp.int32, (NC, NC), 0) == lax.broadcasted_iota(jnp.int32, (NC, NC), 1)
        for r in range(NC):
            row = jnp.broadcast_to(scales_ref[r], (NC, NC))
            column = jnp.sum(jnp.where(eye, row, 0.0), axis=-1, keepdims=True)
            scb[r] = jnp.broadcast_to(0.5 * column, (NC, R))

    def teacher_rows(r, carry):
        codes_copy(r).wait()
        sc = scb[r]
        dT[r] = jnp.zeros((R, E), F32)
        dI[r // 2, r % 2] = jnp.zeros((R, E), F32)

        def some(g, inner):
            for u in range(32):
                i = r * R + g * 32 + u
                pt[pl.ds(i, NC, stride=PITCH), :] = jnp.tanh(codes[i].astype(F32) * sc)
            return inner

        return lax.fori_loop(0, R // 32, some, carry)

    half_scale = 0.5 * scale_ref[0]
    half_bias = 0.5 * bias_ref[0]

    def pairs(zb, hb, count):
        rows = J[zb].reshape(2 * R, E)
        columns = pl.ds(hb * NH, count)
        texts = T[columns].reshape(count * R, E)
        score = lax.dot_general(rows, texts, (((1,), (1,)), ((), ())), preferred_element_type=F32)
        parts = []
        for a in range(2):
            first = hb * (NH * PITCH) + (a * NZ + zb) * R
            cells = []
            for c in range(count):
                teacher = pt[pl.ds(pl.multiple_of(first + c * PITCH, 8), R), :]
                s = score[a * R:(a + 1) * R, c * R:(c + 1) * R]
                cells.append((jnp.tanh(s * half_scale + half_bias) - teacher).astype(BF))
            parts.append(jnp.concatenate(cells, axis=1))
        weight = jnp.concatenate(parts, axis=0)
        part = jnp.dot(weight, texts, preferred_element_type=F32).reshape(2, R, E)
        dI[zb] = part if count == NC else dI[zb] + part
        dT[columns] += lax.dot_general(
            weight, rows, (((0,), (0,)), ((), ())), preferred_element_type=F32
        ).reshape(count, R, E)

    def chip_sum(i, rows):
        hh, dx = SPOTS[i]
        return dT[blk(hcol(hh), x + dx, k), rows] + dr[i, rows].astype(F32)

    def arrived(name, rows):
        _, into, i, _ = landing(name)
        return into[i, rows].astype(F32)

    def send(name):
        needs = NEEDS.get(name, ())
        arrive(needs)
        base, rows = split(name)
        kind = base[0]
        value = None
        if kind in "qrk":
            dz, other = SUMS[base]
            value = dI[zz(dz), lcol(other), rows]
        elif kind == "d":
            hh, dx = SPOTS[int(base[1])]
            value = dT[blk(hcol(hh), x + dx, 1 - k), rows]
        elif kind in "uv":
            value = chip_sum(4 * int(base[1]) + X_SPOTS[kind + base[2]], rows)
        elif kind == "f":
            value = chip_sum(4, rows)
        if value is not None:
            for other in needs:
                if other[0] != "d":
                    value = value + arrived(other, rows)
            out, _, i, _ = landing(name)
            out[i, rows] = value.astype(BF)
        copy(name).start()

    before, events = [], {0: []}
    for item in SCHEDULE:
        if not isinstance(item, str):
            events[len(events)] = []
        elif len(events) == 1:
            before.append(item)
        else:
            events[len(events) - 1].append(item)

    pl.semaphore_wait(barrier, len(partners))
    done = 0
    for n, name in enumerate(before):
        if name != "T":
            send(name)
        elif n + 1 == len(before) or before[n + 1] != "T":
            first, run = done, 1
            while run <= n and before[n - run] == "T":
                run += 1
            done = first + run
            if first == 0:
                teacher_scales()
            lax.fori_loop(first, done, teacher_rows, 0)

    def step(s, carry):
        for n, (hh, d) in enumerate(TILES):
            names = events[n] if n else ()
            texts = TEXTS[hh] if hh < 2 else TEXTS[0] + TEXTS[1]
            waits = tuple(w for w in IMAGES[d] + texts if w not in seen)
            if names or waits:

                def event(names=names, waits=waits):
                    for name in names:
                        send(name)
                    arrive(waits)

                pl.when(s == n)(event)
        zb, hb, full = jnp.int32(0), jnp.int32(0), jnp.int32(0)
        for n, (hh, d) in enumerate(TILES):
            zb = jnp.where(s == n, zz(d), zb)
            if hh < 2:
                hb = jnp.where(s == n, hcol(hh), hb)
            else:
                full = jnp.where(s == n, 1, full)
        pl.when(full == 0)(lambda: pairs(zb, hb, NH))
        pl.when(full == 1)(lambda: pairs(zb, 0, NC))
        return carry

    lax.fori_loop(0, len(TILES), step, 0)
    for name in events[len(TILES)]:
        send(name)

    late = COPIES[-16:]
    for name in COPIES:
        if name not in late:
            copy(name).wait_send()

    whole = pl.ds(0, R)
    unit, mag = unit_rows(txt_ref[...].astype(F32))
    arrive(LAST_TEXT)
    grad = chip_sum(0, whole)
    for name in sorted({split(n)[0] for n in LAST_TEXT if n[0] != "d"}):
        grad = grad + arrived(name, whole)
    dtxt_ref[...] = unit_grad(half_scale * grad, unit, mag)

    unit, mag = unit_rows(img_ref[...].astype(F32))
    arrive(LAST_IMAGE)
    grad = dI[z, l] + arrived("k3", whole) + arrived("q3", whole) + arrived("r3", whole)
    dimg_ref[...] = unit_grad(half_scale * grad, unit, mag)

    for name in late:
        copy(name).wait_send()


def shards(images, texts, teacher_codes, teacher_scales, student_logit_scale, logit_bias):
    vmem = pl.BlockSpec(memory_space=pltpu.VMEM)
    smem = pl.BlockSpec(memory_space=pltpu.SMEM)
    hbm = pl.BlockSpec(memory_space=pl.ANY)
    row = lambda *n: pltpu.VMEM((*n, R, E), BF)
    dma = lambda n: pltpu.SemaphoreType.DMA((n,))
    out = pltpu.VMEM((R, E), F32)
    return pl.pallas_call(
        kernel,
        out_shape=(out, out),
        in_specs=[hbm, hbm, hbm, vmem, smem, smem],
        out_specs=(vmem, vmem),
        scratch_shapes=[
            pltpu.VMEM((NC * R, NC, R), BF),
            pltpu.VMEM((NC, NC, R), F32),
            pltpu.VMEM((NC * PITCH, R), F32),
            row(NZ, 2),
            row(NC),
            pltpu.VMEM((NZ, 2, R, E), F32),
            pltpu.VMEM((NC, R, E), F32),
            row(12), row(12), row(4), row(4), row(8), row(8), row(8), row(8), row(1), row(1),
            row(), row(), dma(2),
            dma(NC), dma(len(COPIES)), dma(len(COPIES)),
        ],
        compiler_params=pltpu.CompilerParams(
            collective_id=0, has_side_effects=True, vmem_limit_bytes=54 * 1024 * 1024
        ),
    )(images, texts, teacher_codes, jnp.swapaxes(teacher_scales, 1, 2), student_logit_scale, logit_bias)


def solution(mesh):
    in_specs = (
        P(("blk", "tile"), None),
        P(("blk", "tile"), None),
        P("blk", None, "tile"),
        P("blk", None, "tile"),
        P(),
        P(),
    )
    out_specs = (P(("blk", "tile"), None), P(("blk", "tile"), None))
    return jax.shard_map(shards, mesh=mesh, in_specs=in_specs, out_specs=out_specs, check_vma=False)
```
